256 devices in a mesh: section: 32 (over x, z_lo, core), dp: 8 (over z_hi, y).
Axes of the slice: x: 4, y: 4, z: 8 (z_hi: 2, z_lo: 4; z = z_hi * 4 + z_lo), core: 2. Of those that a mesh axis runs over, the one named last changes fastest.
Arguments:
- inputs: bfloat16 [4, 256, 2560], P(None, 'dp'), may hold values from -6 to 6
- cotangent: bfloat16 [4, 256, 2560], P(None, 'dp'), may hold values from -6 to 6
- weight: bfloat16 [32, 2560, 2560], P('section', 'dp'), may hold values from -5 to 5
- a_inv: bfloat16 [32, 40, 64, 64], P('section', 'dp'), may hold values from -0.15 to 2, as said below
- g_inv: bfloat16 [32, 40, 64, 64], P('section'), may hold values from -0.15 to 2, as said below
Outputs:
- new_weight: bfloat16 [32, 2560, 2560], P('section', 'dp')
- a_fac: float32 [32, 40, 64, 64], P('section')
- g_fac: float32 [32, 40, 64, 64], P('section')
The draws below stay inside these ranges and needn't reach their ends.
Inputs may be any that keep to these rules, and one draw needn't show every extreme that they name: `a_inv`: blocks of the previous step's inverse factors: positive diagonal, off-diagonal entries small but independent. `g_inv`: blocks of the previous step's inverse factors: positive diagonal, off-diagonal entries small but independent.
All inputs are finite; a program needn't handle non-finite values.
Results may differ from the reference program's by a relative error of at most 0.017.
Values may be sent and summed in bfloat16 or wider, within the bound.
A program may use at most 64 MiB of HBM per device.

```python
import math
import jax
import jax.numpy as jnp
from jax import lax

WD = 2560
BLK = 64
NB = 40
MICRO = 4
TOKENS = 256
SECTIONS = 32


def inverse_blocks(key, low, high):
    key_diag, key_off = jax.random.split(key)
    diagonal = jax.random.uniform(key_diag, (SECTIONS, NB, BLK), jnp.float32, low, high)
    spread = jax.random.normal(key_off, (SECTIONS, NB, BLK, BLK), jnp.float32) * (0.35 / math.sqrt(BLK))
    spread = jnp.clip(spread, -0.149, 0.149)
    identity = jnp.eye(BLK, dtype=jnp.float32)
    return spread * (1.0 - identity) + diagonal[..., None] * identity


def draw_a_inv(key, part):
    key = jax.random.fold_in(key, 11)
    return inverse_blocks(key, 0.5, 1.5).astype(jnp.bfloat16)


def draw_g_inv(key, part):
    key = jax.random.fold_in(key, 23)
    return inverse_blocks(key, 0.5, 1.5).astype(jnp.bfloat16)


def shard_levels(stream_key, shape, pieces, least, largest):
    factor_of = 1.0
    for position, shards_of in pieces:
        heights = jax.random.uniform(jax.random.fold_in(jax.random.fold_in(stream_key, 6), position), (shards_of,), jnp.float32, least / len(pieces), largest / len(pieces))
        factor_of = factor_of * jnp.repeat(jnp.exp(heights), shape[position] // shards_of).reshape((-1,) + (1,) * (len(shape) - 1 - position))
    return factor_of


def centred(key, shape, scale, most, shards=(), kind=jnp.bfloat16):
    drawn = jax.random.normal(key, shape, jnp.float32) * scale
    if len(shards) > 0:
        drawn = shard_levels(key, shape, shards, -0.22, 0.18) * drawn
    return jnp.clip(drawn, min=-most, max=most).astype(kind)


def setup_inputs(seed: int = 0) -> dict:
    streams_of = jax.random.split(jax.random.key(seed), 6)
    return {
        "inputs": centred(streams_of[0], (MICRO, TOKENS, WD), 1.0, 6.0, ((1, 8),)),
        "cotangent": centred(streams_of[1], (MICRO, TOKENS, WD), 1.0, 6.0, ((1, 8),)),
        "weight": centred(streams_of[2], (SECTIONS, WD, WD), 1.0, 5.0, ((0, 32), (1, 8))),
        "a_inv": draw_a_inv(jax.random.fold_in(streams_of[5], 71), 0),
        "g_inv": draw_g_inv(jax.random.fold_in(streams_of[5], 71), 0),
    }


def reference(inputs, cotangent, weight, a_inv, g_inv):
    layer_scale = 0.25 / math.sqrt(WD)
    token_total = MICRO * TOKENS
    start_rows = inputs.reshape(MICRO * TOKENS, WD)
    end_rows = cotangent.reshape(MICRO * TOKENS, WD)

    def forward_section(values, layer_weight):
        product = jnp.dot(values, layer_weight, preferred_element_type=jnp.float32)
        result = (values.astype(jnp.float32) + layer_scale * product).astype(jnp.bfloat16)
        return (result, values)

    def backward_section(values, layer_weight):
        product = jnp.dot(values, layer_weight.T, preferred_element_type=jnp.float32)
        result = (values.astype(jnp.float32) + layer_scale * product).astype(jnp.bfloat16)
        return (result, values)
    _, section_inputs = lax.scan(forward_section, start_rows, weight)
    _, section_cotangents = lax.scan(backward_section, end_rows, weight, reverse=True)

    def factor_blocks(values):
        grouped = values.astype(jnp.float32).reshape(-1, NB, BLK)
        summed = jnp.einsum('rnb,rnc->nbc', grouped, grouped, precision=lax.Precision.HIGHEST)
        return summed / token_total

    def update_section(operands):
        acts, cotans, layer_weight, left_inv, right_inv = operands
        gradient = jnp.dot(acts.T, cotans, preferred_element_type=jnp.float32) / token_total
        reshaped = gradient.reshape(NB, BLK, NB, BLK)
        left_side = jnp.einsum('bij,bjnk->bink', left_inv.astype(jnp.float32), reshaped, precision=lax.Precision.HIGHEST)
        precond = jnp.einsum('bink,nkl->binl', left_side, right_inv.astype(jnp.float32), precision=lax.Precision.HIGHEST)
        updated = (layer_weight.astype(jnp.float32) - precond.reshape(WD, WD)).astype(jnp.bfloat16)
        return (updated, factor_blocks(acts), factor_blocks(cotans))
    new_weight, a_fac, g_fac = lax.map(update_section, (section_inputs, section_cotangents, weight, a_inv, g_inv))
    return (new_weight, a_fac, g_fac)
```

```python
import functools
import math

import jax
import jax.numpy as jnp
from jax import lax
from jax.experimental import pallas as pl
from jax.experimental.pallas import tpu as pltpu
from jax.sharding import PartitionSpec as P

MESH = pl.DeviceIdType.MESH
F32 = jnp.float32
BF16 = jnp.bfloat16
WD = 2560
HALF = WD // 2
ROWS = WD // 8
BLK = 64
NB = 40
WIN = 384
MICRO = 8
M = 32
GROUP = MICRO * M
TOK = 4 * GROUP
SCALE = 0.25 / math.sqrt(WD)
SECTIONS = 32


def lanes(start, size):
    return pl.ds(pl.multiple_of(start, 128), size)


def rows(start, size):
    return pl.ds(pl.multiple_of(start, 64), size)


def kernel(
    x_in, c_in, w_in, a_inv, g_inv,
    w_out, a_out, g_out,
    full_w, half_w, near, far, whole, half_in, half_out, part_out, acc,
    x_win, c_all, x_t,
    gat_send, gat_recv, start_send, start_recv,
    near_send, near_recv, far_send, far_recv, half_send, half_recv,
    ex_send, ex_recv, fac_send, fac_recv,
):
    section = lax.axis_index("section")
    dp = lax.axis_index("dp")
    core = lax.rem(section, 2)
    pair = section // 2
    hi = dp // 4
    y = lax.rem(dp, 4)
    other_hi = 1 - hi
    beside = 4 * other_hi + y
    mate = section + 1 - 2 * core
    outer = section - 1 + 2 * core
    at_end = jnp.logical_or(outer < 0, outer >= SECTIONS)
    even = core == 0
    mine = lanes(hi * HALF, HALF)
    others = lanes(other_hi * HALF, HALF)

    def across(step):
        return lax.rem(y + step, 4)

    def copy(src, dst, send, recv, target):
        return pltpu.make_async_remote_copy(
            src_ref=src, dst_ref=dst, send_sem=send, recv_sem=recv,
            device_id=target, device_id_type=MESH,
        )

    barrier = pltpu.get_barrier_semaphore()

    def greet(target):
        pl.semaphore_signal(barrier, inc=1, device_id=target, device_id_type=MESH)

    for step in (1, 2, 3):
        greet((section, 4 * hi + across(step)))
        greet((section, 4 * other_hi + across(step)))
    greet((section, beside))
    greet((mate, dp))

    @pl.when(jnp.logical_not(at_end))
    def _():
        greet((outer, dp))
        greet((outer, beside))
        pl.semaphore_wait(barrier, 10)

    @pl.when(at_end)
    def _():
        pl.semaphore_wait(barrier, 8)

    def piece(owner):
        return full_w.at[rows(owner * ROWS, ROWS), :]

    def strip(owner_y):
        return half_w.at[rows(owner_y * ROWS, ROWS), :]

    @pl.when(even)
    def _():
        side = copy(w_in.at[:, others], piece(dp), gat_send.at[6], gat_recv.at[6], (section, beside))
        side.start()
        sends = []
        for step in (1, 2, 3):
            sends.append(copy(
                w_in.at[:, mine], piece(dp), gat_send.at[step - 1], gat_recv.at[step - 1],
                (section, 4 * hi + across(step)),
            ))
            sends[-1].start()
        full_w[rows(dp * ROWS, ROWS), :] = w_in[:, mine]
        side.wait_recv()
        for step in (1, 2, 3):
            sends.append(copy(
                piece(beside), piece(beside), gat_send.at[step + 2], gat_recv.at[step + 2],
                (section, 4 * hi + across(step)),
            ))
            sends[-1].start()
        for one in sends:
            one.wait_recv()

        @pl.loop(0, 10)
        def _(i):
            half_w[:, lanes(i * 256, 256)] = full_w[rows(i * 256, 256), :].T

        side.wait_send()
        for one in sends:
            one.wait_send()

    @pl.when(jnp.logical_not(even))
    def _():
        sends = []
        for step in (1, 2, 3):
            sends.append(copy(
                w_in, strip(y), gat_send.at[step - 1], gat_recv.at[step - 1],
                (section, 4 * hi + across(step)),
            ))
            sends[-1].start()
        half_w[rows(y * ROWS, ROWS), :] = w_in[...]
        for one in sends:
            one.wait_recv()

        @pl.loop(0, 10)
        def _(i):
            full_w[rows(i * 256, 256), :] = half_w[:, lanes(i * 256, 256)].T

        for one in sends:
            one.wait_send()

    def begin(source):
        own = copy(source, whole.at[pl.ds(4 * hi, 4)], start_send, start_recv, (section, beside))
        own.start()
        whole[pl.ds(4 * hi, 4)] = source[...]
        own.wait()

    @pl.when(jnp.logical_and(at_end, even))
    def _():
        begin(x_in)

    @pl.when(jnp.logical_and(at_end, jnp.logical_not(even)))
    def _():
        begin(c_in)

    def to_mate(k):
        return copy(half_out.at[k], half_in.at[k], half_send.at[k], half_recv.at[k], (mate, dp))

    def to_near(k):
        return copy(part_out.at[k], near.at[k], near_send.at[k], near_recv.at[k], (outer, dp))

    def to_far(k):
        return copy(part_out.at[k], far.at[k], far_send.at[k], far_recv.at[k], (outer, beside))

    def from_whole():
        @pl.loop(0, MICRO)
        def _(k):
            @pl.when(jnp.logical_not(at_end))
            def _():
                to_near(k).wait_recv()
                to_far(k).wait_recv()
                whole[k] = (near[k].astype(F32) + far[k].astype(F32)).astype(BF16)

            for n in range(5):
                acc[:, n * 256:(n + 1) * 256] = jnp.dot(
                    whole[k], full_w[:, n * 256:(n + 1) * 256], preferred_element_type=F32
                )
            half_out[k] = (whole[k, :, mine].astype(F32) + SCALE * acc[:, :HALF]).astype(BF16)
            to_mate(k).start()

    def from_half():
        @pl.loop(0, MICRO)
        def _(k):
            to_mate(k).wait_recv()
            for n in range(5):
                acc[:, n * 512:(n + 1) * 512] = jnp.dot(
                    half_in[k], half_w[:, n * 512:(n + 1) * 512], preferred_element_type=F32
                )
            part_out[k] = (SCALE * acc[...]).astype(BF16)
            part_out[k, :, mine] = (half_in[k].astype(F32) + SCALE * acc[:, mine]).astype(BF16)

            @pl.when(jnp.logical_not(at_end))
            def _():
                to_near(k).start()
                to_far(k).start()

    whole_first = (pair < SECTIONS // 4) == even

    @pl.when(whole_first)
    def _():
        from_whole()

    from_half()

    @pl.when(jnp.logical_not(whole_first))
    def _():
        from_whole()

    def window(owner):
        return 320 * owner - 64 * lax.rem(owner, 2)

    spread = []

    def exchange_window(source, slot):
        sends = []
        for step in (1, 2, 3):
            to = across(step)
            sends.append(copy(
                source(to), x_win.at[y], ex_send.at[step - 1], ex_recv.at[step - 1],
                (section, 4 * hi + to),
            ))
            sends[-1].start()
        return sends

    @pl.when(even)
    def _():
        def view(to):
            return whole.at[:, :, lanes(window(4 * hi + to), WIN)]

        sends = exchange_window(view, None)
        x_win[y] = whole[:, :, lanes(window(dp), WIN)]
        side = copy(
            half_in, c_all.at[y, :, :, mine], ex_send.at[9], ex_recv.at[9], (section, beside)
        )
        side.start()
        for step in (1, 2, 3):
            sends.append(copy(
                half_in, c_all.at[y, :, :, mine], ex_send.at[step + 2], ex_recv.at[step + 2],
                (section, 4 * hi + across(step)),
            ))
            sends[-1].start()
        c_all[y, :, :, mine] = half_in[...]
        side.wait_recv()
        for step in (1, 2, 3):
            sends.append(copy(
                c_all.at[y, :, :, others], c_all.at[y, :, :, others],
                ex_send.at[step + 5], ex_recv.at[step + 5], (section, 4 * hi + across(step)),
            ))
            sends[-1].start()
        for one in sends:
            one.wait_recv()
        side.wait_send()
        for one in sends:
            one.wait_send()

    @pl.when(jnp.logical_not(even))
    def _():
        def view(to):
            return half_in.at[:, :, lanes(window(to), WIN)]

        sends = exchange_window(view, None)
        x_win[y] = half_in[:, :, lanes(window(y), WIN)]
        for step in (1, 2, 3):
            sends.append(copy(
                whole, c_all.at[y], ex_send.at[step + 2], ex_recv.at[step + 2],
                (section, 4 * hi + across(step)),
            ))
            sends[-1].start()
        c_all[y] = whole[...]
        for one in sends:
            one.wait()

    for g in range(4):
        x_t[:, g * GROUP:(g + 1) * GROUP] = x_win[g].reshape(GROUP, WIN).T
    own_rows = rows(64 * lax.rem(y, 2), ROWS)

    def select(height, width):
        return (
            lax.rem(lax.broadcasted_iota(jnp.int32, (height, width), 0), 64)
            == lax.rem(lax.broadcasted_iota(jnp.int32, (height, width), 1), 64)
        )

    def same_block(size):
        return (
            lax.broadcasted_iota(jnp.int32, (size, size), 0) // 64
            == lax.broadcasted_iota(jnp.int32, (size, size), 1) // 64
        )

    def fold(gram):
        size = gram.shape[0]
        kept = jnp.where(same_block(size), gram, 0.0)
        return jnp.dot(
            kept, select(size, 64).astype(F32), precision=lax.Precision.HIGHEST,
            preferred_element_type=F32,
        )

    def unfold(blocks):
        size = blocks.shape[0]
        tiled = jnp.dot(blocks, select(64, size).astype(BF16), preferred_element_type=F32)
        return jnp.where(same_block(size), tiled, 0.0).astype(BF16)

    def contract(a, b):
        return lax.dot_general(a, b, (((1,), (1,)), ((), ())), preferred_element_type=F32)

    own = x_t[own_rows, :]
    own_blocks = rows(dp * ROWS, ROWS)
    a_out[own_blocks, :] = fold(contract(own, own) / TOK)
    shares = []
    for index in range(7):
        step = index % 4 if index < 4 else index - 3
        target_hi = other_hi if index < 4 else hi
        one = copy(
            a_out.at[own_blocks, :], a_out.at[own_blocks, :], fac_send.at[index], fac_recv.at[index],
            (section, 4 * target_hi + across(step)),
        )
        one.start()
        shares.append(one)

    left = unfold(a_inv[...])

    @pl.loop(0, 10)
    def _(n):
        cols = lanes(n * 256, 256)
        c_cols = c_all[:, :, :, cols].reshape(TOK, 256)
        g_out[rows(n * 256, 256), :] = fold(jnp.dot(c_cols.T, c_cols, preferred_element_type=F32) / TOK)
        grad = jnp.dot(x_t[own_rows, :], c_cols, preferred_element_type=F32) / TOK
        halfway = jnp.dot(left, grad.astype(BF16), preferred_element_type=F32).astype(BF16)
        right = unfold(g_inv[rows(n * 256, 256), :])
        step = jnp.dot(halfway, right, preferred_element_type=F32)
        w_out[:, cols] = (w_in[:, cols].astype(F32) - step).astype(BF16)

    for one in shares:
        one.wait()

    @pl.loop(0, MICRO)
    def _(k):
        to_mate(k).wait_send()

        @pl.when(jnp.logical_not(at_end))
        def _():
            to_near(k).wait_send()
            to_far(k).wait_send()


def local(inputs, cotangent, weight, a_inv, g_inv):
    vmem = pl.BlockSpec(memory_space=pltpu.VMEM)
    dma = pltpu.SemaphoreType.DMA
    new_weight, a_fac, g_fac = pl.pallas_call(
        kernel,
        out_shape=(
            jax.ShapeDtypeStruct((ROWS, WD), BF16),
            jax.ShapeDtypeStruct((WD, BLK), F32),
            jax.ShapeDtypeStruct((WD, BLK), F32),
        ),
        in_specs=[vmem] * 5,
        out_specs=(vmem,) * 3,
        scratch_shapes=[
            pltpu.VMEM((WD, HALF), BF16),
            pltpu.VMEM((HALF, WD), BF16),
            pltpu.VMEM((MICRO, M, WD), BF16),
            pltpu.VMEM((MICRO, M, WD), BF16),
            pltpu.VMEM((MICRO, M, WD), BF16),
            pltpu.VMEM((MICRO, M, HALF), BF16),
            pltpu.VMEM((MICRO, M, HALF), BF16),
            pltpu.VMEM((MICRO, M, WD), BF16),
            pltpu.VMEM((M, WD), F32),
            pltpu.VMEM((4, MICRO, M, WIN), BF16),
            pltpu.VMEM((4, MICRO, M, WD), BF16),
            pltpu.VMEM((WIN, TOK), BF16),
            dma((7,)), dma((7,)), dma, dma,
            dma((MICRO,)), dma((MICRO,)), dma((MICRO,)), dma((MICRO,)),
            dma((MICRO,)), dma((MICRO,)),
            dma((10,)), dma((10,)), dma((7,)), dma((7,)),
        ],
        compiler_params=pltpu.CompilerParams(
            collective_id=0, has_side_effects=True, vmem_limit_bytes=56 << 20
        ),
        cost_estimate=pl.CostEstimate(flops=6 << 30, bytes_accessed=8 << 20, transcendentals=0),
        name="kfac",
    )(
        inputs, cotangent, weight[0],
        a_inv[0].reshape(ROWS, BLK), g_inv[0].reshape(WD, BLK),
    )
    return (
        new_weight[None],
        a_fac.reshape(1, NB, BLK, BLK),
        g_fac.reshape(1, NB, BLK, BLK),
    )


def solution(mesh):
    placed = (
        P(None, "dp", None),
        P(None, "dp", None),
        P("section", "dp", None),
        P("section", "dp", None, None),
        P("section", None, None, None),
    )
    return jax.shard_map(
        local,
        mesh=mesh,
        in_specs=placed,
        out_specs=(
            P("section", "dp", None),
            P("section", None, None, None),
            P("section", None, None, None),
        ),
        check_vma=False,
    )
```

```python
import functools
import math

import jax
import jax.numpy as jnp
from jax import lax
from jax.experimental import pallas as pl
from jax.experimental.pallas import tpu as pltpu
from jax.sharding import PartitionSpec as P

MESH = pl.DeviceIdType.MESH
F32 = jnp.float32
BF16 = jnp.bfloat16
WD = 2560
ROWS = WD // 8
BLK = 64
NB = 40
WIN = 384
MICRO = 4
M = 32
GROUP = MICRO * M
TOK = 8 * GROUP
SCALE = 0.25 / math.sqrt(WD)
SECTIONS = 32
TURN = 8
LAG = 10
CUTS = tuple((start, 512) for start in range(0, WD, 512))


def lanes(start, size):
    return pl.ds(pl.multiple_of(start, 128), size)


def rows(start, size):
    return pl.ds(pl.multiple_of(start, 64), size)


def kernel(
    x_in, c_in, w_in, a_inv, g_inv,
    w_out, a_out, g_out,
    deep_w, wide_w, deep_in, wide_in, deep_out, wide_out, acc,
    x_win, c_all, x_t, fac,
    gat_send, gat_recv, deep_send, deep_recv, wide_send, wide_recv,
    x_send, x_recv, c_send, c_recv, fac_send, fac_recv,
):
    section = lax.axis_index("section")
    dp = lax.axis_index("dp")
    core = lax.rem(section, 2)
    pair = section // 2
    hi = dp // 4
    y = lax.rem(dp, 4)
    other_hi = 1 - hi
    beside = 4 * other_hi + y
    mate = section + 1 - 2 * core
    outer = section - 1 + 2 * core
    at_end = jnp.logical_or(outer < 0, outer >= SECTIONS)
    even = core == 0

    def across(step):
        return lax.rem(y + step, 4)

    def copy(src, dst, send, recv, target):
        return pltpu.make_async_remote_copy(
            src_ref=src, dst_ref=dst, send_sem=send, recv_sem=recv,
            device_id=target, device_id_type=MESH,
        )

    def peer(index):
        if index < 4:
            return (section, 4 * other_hi + across(index))
        return (section, 4 * hi + across(index - 3))

    barrier = pltpu.get_barrier_semaphore()

    def greet(target):
        pl.semaphore_signal(barrier, inc=1, device_id=target, device_id_type=MESH)

    for index in range(7):
        greet(peer(index))
    greet((mate, dp))

    @pl.when(jnp.logical_not(at_end))
    def _():
        greet((outer, dp))
        pl.semaphore_wait(barrier, 9)

    @pl.when(at_end)
    def _():
        pl.semaphore_wait(barrier, 8)

    ahead, behind = across(1), across(3)

    def ring(view, own, send, recv):
        def to(target_y, slot, ref, place):
            return copy(ref, place, send(slot), recv(slot), (section, 4 * hi + target_y))

        def link(slot):
            if slot < 2:
                return to((ahead, behind)[slot], slot, own, view(y))
            passed = view((behind, ahead)[slot - 2], slot - 2)
            return to((ahead, behind)[slot - 2], slot, passed, passed)

        return link

    def pass_on(links):
        links(0).wait_recv()
        links(2).start()
        links(1).wait_recv()
        links(3).start()

    def arrived(links):
        links(2).wait_recv()
        links(3).wait_recv()

    def sent(links):
        for slot in range(4):
            links(slot).wait_send()

    def gather_weight(full, flipped):
        def block(group, low, size):
            def view(owner, part=None):
                start = (4 * group + owner) * ROWS + low
                if part is None:
                    return full.at[pl.ds(pl.multiple_of(start, 32), size), :]
                half = size // 2
                return full.at[pl.ds(pl.multiple_of(start + part * half, 16), half), :]

            return view

        def links_of(view, own, base):
            return ring(
                view, own, lambda slot: gat_send.at[base + slot], lambda slot: gat_recv.at[base + slot]
            )

        half = ROWS // 2
        sides, rings = [], []
        for part in range(2):
            there = block(hi, part * half, half)(y)
            sides.append(copy(
                w_in.at[pl.ds(part * half, half), :], there,
                gat_send.at[12 + part], gat_recv.at[12 + part], (section, beside),
            ))
            sides[-1].start()
        close = links_of(block(hi, 0, ROWS), w_in, 0)
        close(0).start()
        close(1).start()
        full[rows(dp * ROWS, ROWS), :] = w_in[...]
        for part in range(2):
            view = block(other_hi, part * half, half)
            rings.append(links_of(view, view(y), 4 + 4 * part))

        def turn(group):
            for n in range(5):
                cols = lanes(group * 4 * ROWS + n * 256, 256)
                flipped[:, cols] = full[rows(group * 4 * ROWS + n * 256, 256), :].T

        sides[0].wait_recv()
        rings[0](0).start()
        rings[0](1).start()
        pass_on(close)
        sides[1].wait_recv()
        rings[1](0).start()
        rings[1](1).start()
        arrived(close)
        turn(hi)
        pass_on(rings[0])
        pass_on(rings[1])
        arrived(rings[0])
        arrived(rings[1])
        turn(other_hi)
        for one in sides:
            one.wait_send()
        for links in (close, rings[0], rings[1]):
            sent(links)

    @pl.when(even)
    def _():
        gather_weight(deep_w, wide_w)

    @pl.when(jnp.logical_not(even))
    def _():
        gather_weight(wide_w, deep_w)

    @pl.when(jnp.logical_and(at_end, even))
    def _():
        deep_in[...] = x_in[...]

    @pl.when(jnp.logical_and(at_end, jnp.logical_not(even)))
    def _():
        deep_in[...] = c_in[...]

    def to_mate(k):
        return copy(deep_out.at[k], wide_in.at[k], wide_send.at[k], wide_recv.at[k], (mate, dp))

    def to_outer(k, n):
        view = (k, slice(None), pl.ds(*CUTS[n]))
        return copy(
            wide_out.at[view], deep_in.at[view], deep_send.at[k, n], deep_recv.at[k, n], (outer, dp)
        )

    def window(owner):
        return 320 * owner - 64 * lax.rem(owner, 2)

    def x_link(k, index, source):
        return copy(
            source, x_win.at[dp, k], x_send.at[k, index], x_recv.at[k, index], peer(index)
        )

    def send_x(k, source):
        for index in range(7):
            start = window(peer(index)[1])
            x_link(k, index, source.at[k, :, lanes(start, WIN)]).start()
        x_win[dp, k] = source[k, :, lanes(window(dp), WIN)]

    def c_ring(k, group, base):
        def view(owner, part=None):
            if part is None:
                return c_all.at[4 * group + owner, k]
            return c_all.at[4 * group + owner, k, :, pl.ds(part * (WD // 2), WD // 2)]

        return ring(
            view, view(y), lambda slot: c_send.at[k, base + slot], lambda slot: c_recv.at[k, base + slot]
        )

    def c_side(k):
        view = c_all.at[dp, k]
        return copy(view, view, c_send.at[k, 8], c_recv.at[k, 8], (section, beside))

    def send_c(k, source):
        c_all[dp, k] = source[k]
        c_side(k).start()
        links = c_ring(k, hi, 0)
        links(0).start()
        links(1).start()

    def run_deep(k, is_even, is_end):
        for n, (start, size) in enumerate(CUTS):
            if not is_end:
                to_outer(k, n).wait_recv()
            term = jnp.dot(
                deep_in[k, :, start:start + size], deep_w[start:start + size, :],
                preferred_element_type=F32,
            )
            if n == 0:
                acc[...] = term
            else:
                acc[...] += term
        deep_out[k] = (deep_in[k].astype(F32) + SCALE * acc[...]).astype(BF16)
        to_mate(k).start()
        if is_even:
            send_x(k, deep_in)
        else:
            send_c(k, deep_in)

    def run_wide(k, is_even, is_end):
        to_mate(k).wait_recv()
        if not is_end:
            for n, (start, size) in enumerate(CUTS):
                term = jnp.dot(
                    wide_in[k], wide_w[:, start:start + size], preferred_element_type=F32
                )
                kept = wide_in[k, :, start:start + size].astype(F32)
                wide_out[k, :, start:start + size] = (kept + SCALE * term).astype(BF16)
                to_outer(k, n).start()
        if is_even:
            send_c(k, wide_in)
        else:
            send_x(k, wide_in)

    def by_place(work, k, allowed):
        for is_even in (True, False):
            for is_end in (True, False):
                here = jnp.logical_and(even == is_even, at_end == is_end)

                @pl.when(jnp.logical_and(allowed, here))
                def _():
                    work(k, is_even, is_end)

    def each(work):
        @pl.loop(0, MICRO)
        def _(k):
            work(k)

    def gather_c():
        def widen(k):
            c_side(k).wait_recv()
            links = c_ring(k, other_hi, 4)
            links(0).start()
            links(1).start()

        each(widen)
        each(lambda k: pass_on(c_ring(k, hi, 0)))
        each(lambda k: pass_on(c_ring(k, other_hi, 4)))

        def finish(k):
            arrived(c_ring(k, hi, 0))
            arrived(c_ring(k, other_hi, 4))

        each(finish)

    deep_first = (pair < TURN) == even
    early = pair >= 12
    gap = jnp.where(pair < TURN, 2 * TURN - 1 - 2 * pair, 2 * pair + 1 - 2 * TURN)
    lag = jnp.minimum(gap * LAG // 4, MICRO)
    deep_lag = jnp.where(deep_first, 0, lag)
    wide_lag = jnp.where(deep_first, lag, 0)

    @pl.loop(0, MICRO + lag)
    def _(t):
        def turn(work, late):
            k = t - late
            allowed = jnp.logical_and(k >= 0, k < MICRO)
            by_place(work, jnp.clip(k, 0, MICRO - 1), allowed)

        turn(run_deep, deep_lag)
        turn(run_wide, wide_lag)

        @pl.when(jnp.logical_and(early, t == MICRO - 1))
        def _():
            gather_c()

    def take_x(k):
        for index in range(7):
            x_link(k, index, x_win.at[dp, k]).wait_recv()

    each(take_x)

    @pl.when(jnp.logical_not(early))
    def _():
        gather_c()

    for g in range(8):
        x_t[:, g * GROUP:(g + 1) * GROUP] = x_win[g].reshape(GROUP, WIN).T
    own_rows = rows(64 * lax.rem(y, 2), ROWS)

    def select(height, width):
        return (
            lax.rem(lax.broadcasted_iota(jnp.int32, (height, width), 0), 64)
            == lax.broadcasted_iota(jnp.int32, (height, width), 1)
        )

    def same_block(size):
        return (
            lax.broadcasted_iota(jnp.int32, (size, size), 0) // 64
            == lax.broadcasted_iota(jnp.int32, (size, size), 1) // 64
        )

    def fold(gram, width=64):
        size = gram.shape[0]
        kept = jnp.where(same_block(size), gram, 0.0)
        return jnp.dot(
            kept, select(size, width).astype(F32), precision=lax.Precision.HIGHEST,
            preferred_element_type=F32,
        )

    def unfold(blocks):
        size = blocks.shape[0]
        tiled = lax.dot_general(
            blocks, select(size, 64).astype(BF16), (((1,), (1,)), ((), ())), preferred_element_type=F32
        )
        return jnp.where(same_block(size), tiled, 0.0).astype(BF16)

    def contract(a, b):
        return lax.dot_general(a, b, (((1,), (1,)), ((), ())), preferred_element_type=F32)

    own = x_t[own_rows, :]
    fac[dp] = fold(contract(own, own) / TOK, 128).astype(BF16)
    shares = []
    for index in range(7):
        one = copy(
            fac.at[dp], fac.at[dp], fac_send.at[index], fac_recv.at[index], peer(index)
        )
        one.start()
        shares.append(one)

    left = unfold(a_inv[...])

    @pl.loop(0, 10)
    def _(n):
        cols = lanes(n * 256, 256)
        c_cols = c_all[:, :, :, cols].reshape(TOK, 256)
        g_out[rows(n * 256, 256), :] = fold(jnp.dot(c_cols.T, c_cols, preferred_element_type=F32) / TOK)
        grad = jnp.dot(x_t[own_rows, :], c_cols, preferred_element_type=F32) / TOK
        halfway = jnp.dot(left, grad.astype(BF16), preferred_element_type=F32).astype(BF16)
        right = unfold(g_inv[rows(n * 256, 256), :])
        step = jnp.dot(halfway, right, preferred_element_type=F32)
        w_out[:, cols] = (w_in[:, cols].astype(F32) - step).astype(BF16)

    for one in shares:
        one.wait()
    for owner in range(8):
        a_out[owner * ROWS:(owner + 1) * ROWS, :] = fac[owner, :, :BLK].astype(F32)

    def close_sends(k):
        to_mate(k).wait_send()
        for index in range(7):
            x_link(k, index, x_win.at[dp, k]).wait_send()

        @pl.when(jnp.logical_not(at_end))
        def _():
            for n in range(len(CUTS)):
                to_outer(k, n).wait_send()

        c_side(k).wait_send()
        sent(c_ring(k, hi, 0))
        sent(c_ring(k, other_hi, 4))

    each(close_sends)


def local(inputs, cotangent, weight, a_inv, g_inv):
    vmem = pl.BlockSpec(memory_space=pltpu.VMEM)
    dma = pltpu.SemaphoreType.DMA
    held = pltpu.VMEM((MICRO, M, WD), BF16)
    new_weight, a_fac, g_fac = pl.pallas_call(
        kernel,
        out_shape=(
            jax.ShapeDtypeStruct((ROWS, WD), BF16),
            jax.ShapeDtypeStruct((WD, BLK), F32),
            jax.ShapeDtypeStruct((WD, BLK), F32),
        ),
        in_specs=[vmem] * 5,
        out_specs=(vmem,) * 3,
        scratch_shapes=[
            pltpu.VMEM((WD, WD), BF16),
            pltpu.VMEM((WD, WD), BF16),
            held, held, held, held,
            pltpu.VMEM((M, WD), F32),
            pltpu.VMEM((8, MICRO, M, WIN), BF16),
            pltpu.VMEM((8, MICRO, M, WD), BF16),
            pltpu.VMEM((WIN, TOK), BF16),
            pltpu.VMEM((8, ROWS, 128), BF16),
            dma((14,)), dma((14,)),
            dma((MICRO, len(CUTS))), dma((MICRO, len(CUTS))), dma((MICRO,)), dma((MICRO,)),
            dma((MICRO, 7)), dma((MICRO, 7)), dma((MICRO, 9)), dma((MICRO, 9)),
            dma((7,)), dma((7,)),
        ],
        compiler_params=pltpu.CompilerParams(
            collective_id=0, has_side_effects=True, vmem_limit_bytes=56 << 20
        ),
        cost_estimate=pl.CostEstimate(flops=6 << 30, bytes_accessed=8 << 20, transcendentals=0),
        name="kfac",
    )(
        inputs, cotangent, weight[0],
        a_inv[0].reshape(ROWS, BLK), g_inv[0].reshape(WD, BLK),
    )
    return (
        new_weight[None],
        a_fac.reshape(1, NB, BLK, BLK),
        g_fac.reshape(1, NB, BLK, BLK),
    )


def solution(mesh):
    placed = (
        P(None, "dp", None),
        P(None, "dp", None),
        P("section", "dp", None),
        P("section", "dp", None, None),
        P("section", None, None, None),
    )
    return jax.shard_map(
        local,
        mesh=mesh,
        in_specs=placed,
        out_specs=(
            P("section", "dp", None),
            P("section", None, None, None),
            P("section", None, None, None),
        ),
        check_vma=False,
    )
```

```python
import functools
import math

import jax
import jax.numpy as jnp
from jax import lax
from jax.experimental import pallas as pl
from jax.experimental.pallas import tpu as pltpu
from jax.sharding import PartitionSpec as P

MESH = pl.DeviceIdType.MESH
F32 = jnp.float32
BF16 = jnp.bfloat16
WD = 2560
ROWS = WD // 8
BLK = 64
NB = 40
WIN = 384
MICRO = 4
M = 32
GROUP = MICRO * M
TOK = 8 * GROUP
SCALE = 0.25 / math.sqrt(WD)
SECTIONS = 32
TURN = 8
LAG = 10
TELL = 2
CUTS = tuple((start, 512) for start in range(0, WD, 512))


def lanes(start, size):
    return pl.ds(pl.multiple_of(start, 128), size)


def rows(start, size):
    return pl.ds(pl.multiple_of(start, 64), size)


def kernel(
    x_in, c_in, w_in, a_inv, g_inv,
    w_out, a_out, g_out,
    deep_w, wide_w, deep_in, wide_in, deep_out, wide_out, acc,
    x_win, c_all, x_t, fac,
    gat_send, gat_recv, deep_send, deep_recv, wide_send, wide_recv,
    x_send, x_recv, c_send, c_recv, fac_send, fac_recv, passed,
):
    section = lax.axis_index("section")
    dp = lax.axis_index("dp")
    core = lax.rem(section, 2)
    pair = section // 2
    plane = section // 8
    early = plane == 3
    middle = jnp.logical_and(plane > 0, plane < 3)
    hi = dp // 4
    y = lax.rem(dp, 4)
    other_hi = 1 - hi
    beside = 4 * other_hi + y
    mate = section + 1 - 2 * core
    outer = section - 1 + 2 * core
    at_end = jnp.logical_or(outer < 0, outer >= SECTIONS)
    even = core == 0

    def across(step):
        return lax.rem(y + step, 4)

    def copy(src, dst, send, recv, target):
        return pltpu.make_async_remote_copy(
            src_ref=src, dst_ref=dst, send_sem=send, recv_sem=recv,
            device_id=target, device_id_type=MESH,
        )

    def peer(index):
        if index < 4:
            return (section, 4 * other_hi + across(index))
        return (section, 4 * hi + across(index - 3))

    barrier = pltpu.get_barrier_semaphore()

    def greet(target):
        pl.semaphore_signal(barrier, inc=1, device_id=target, device_id_type=MESH)

    for index in range(7):
        greet(peer(index))
    greet((mate, dp))
    teller = jnp.where(plane == 0, 8, jnp.where(plane == 1, 7, jnp.where(plane == 2, 24, 23)))
    telling = jnp.logical_or(
        jnp.logical_or(section == 7, section == 8), jnp.logical_or(section == 23, section == 24)
    )

    @pl.when(teller != outer)
    def _():
        greet((teller, dp))

    @pl.when(jnp.logical_not(at_end))
    def _():
        greet((outer, dp))

    pl.semaphore_wait(barrier, 8 + jnp.where(at_end, 0, 1) + jnp.where(telling, 7, 0))

    ahead, behind = across(1), across(3)

    def ring(view, own, send, recv):
        def to(target_y, slot, ref, place):
            return copy(ref, place, send(slot), recv(slot), (section, 4 * hi + target_y))

        def link(slot):
            if slot < 2:
                return to((ahead, behind)[slot], slot, own, view(y))
            passed = view((behind, ahead)[slot - 2], slot - 2)
            return to((ahead, behind)[slot - 2], slot, passed, passed)

        return link

    def pass_on(links):
        links(0).wait_recv()
        links(2).start()
        links(1).wait_recv()
        links(3).start()

    def arrived(links):
        links(2).wait_recv()
        links(3).wait_recv()

    def sent(links):
        for slot in range(4):
            links(slot).wait_send()

    def gather_weight(full, flipped):
        def block(group, low, size):
            def view(owner, part=None):
                start = (4 * group + owner) * ROWS + low
                if part is None:
                    return full.at[pl.ds(pl.multiple_of(start, 32), size), :]
                half = size // 2
                return full.at[pl.ds(pl.multiple_of(start + part * half, 16), half), :]

            return view

        def links_of(view, own, base):
            return ring(
                view, own, lambda slot: gat_send.at[base + slot], lambda slot: gat_recv.at[base + slot]
            )

        half = ROWS // 2
        sides, rings = [], []
        for part in range(2):
            there = block(hi, part * half, half)(y)
            sides.append(copy(
                w_in.at[pl.ds(part * half, half), :], there,
                gat_send.at[12 + part], gat_recv.at[12 + part], (section, beside),
            ))
            sides[-1].start()
        close = links_of(block(hi, 0, ROWS), w_in, 0)
        close(0).start()
        close(1).start()
        full[rows(dp * ROWS, ROWS), :] = w_in[...]
        for part in range(2):
            view = block(other_hi, part * half, half)
            rings.append(links_of(view, view(y), 4 + 4 * part))

        def turn(group):
            for n in range(5):
                cols = lanes(group * 4 * ROWS + n * 256, 256)
                flipped[:, cols] = full[rows(group * 4 * ROWS + n * 256, 256), :].T

        sides[0].wait_recv()
        rings[0](0).start()
        rings[0](1).start()
        pass_on(close)
        sides[1].wait_recv()
        rings[1](0).start()
        rings[1](1).start()
        arrived(close)
        turn(hi)
        pass_on(rings[0])
        pass_on(rings[1])
        arrived(rings[0])
        arrived(rings[1])
        turn(other_hi)
        for one in sides:
            one.wait_send()
        for links in (close, rings[0], rings[1]):
            sent(links)

    @pl.when(even)
    def _():
        gather_weight(deep_w, wide_w)

    @pl.when(jnp.logical_not(even))
    def _():
        gather_weight(wide_w, deep_w)

    @pl.when(jnp.logical_and(at_end, even))
    def _():
        deep_in[...] = x_in[...]

    @pl.when(jnp.logical_and(at_end, jnp.logical_not(even)))
    def _():
        deep_in[...] = c_in[...]

    def to_mate(k):
        return copy(deep_out.at[k], wide_in.at[k], wide_send.at[k], wide_recv.at[k], (mate, dp))

    def to_outer(k, n):
        view = (k, slice(None), pl.ds(*CUTS[n]))
        return copy(
            wide_out.at[view], deep_in.at[view], deep_send.at[k, n], deep_recv.at[k, n], (outer, dp)
        )

    def window(owner):
        return 320 * owner - 64 * lax.rem(owner, 2)

    def x_link(index, source):
        return copy(source, x_win.at[dp], x_send.at[index], x_recv.at[index], peer(index))

    def send_x(source):
        for index in range(7):
            start = window(peer(index)[1])
            x_link(index, source.at[:, :, lanes(start, WIN)]).start()
        x_win[dp] = source[:, :, lanes(window(dp), WIN)]

    def send_own_x():
        @pl.when(even)
        def _():
            send_x(deep_in)

        @pl.when(jnp.logical_not(even))
        def _():
            send_x(wide_in)

    def c_ring(k, group, base):
        def view(owner, part=None):
            if part is None:
                return c_all.at[4 * group + owner, k]
            return c_all.at[4 * group + owner, k, :, pl.ds(part * (WD // 2), WD // 2)]

        return ring(
            view, view(y), lambda slot: c_send.at[k, base + slot], lambda slot: c_recv.at[k, base + slot]
        )

    def c_side(k):
        view = c_all.at[dp, k]
        return copy(view, view, c_send.at[k, 8], c_recv.at[k, 8], (section, beside))

    def send_c(k, source):
        c_all[dp, k] = source[k]
        links = c_ring(k, hi, 0)
        links(0).start()
        links(1).start()

        @pl.when(plane == 0)
        def _():
            c_side(k).start()

    def widen(k):
        c_side(k).wait_recv()
        links = c_ring(k, other_hi, 4)
        links(0).start()
        links(1).start()

    def pass_close(k):
        pass_on(c_ring(k, hi, 0))

    def run_deep(k, is_even, is_end):
        for n, (start, size) in enumerate(CUTS):
            if not is_end:
                to_outer(k, n).wait_recv()
            term = jnp.dot(
                deep_in[k, :, start:start + size], deep_w[start:start + size, :],
                preferred_element_type=F32,
            )
            if n == 0:
                acc[...] = term
            else:
                acc[...] += term
        deep_out[k] = (deep_in[k].astype(F32) + SCALE * acc[...]).astype(BF16)
        to_mate(k).start()
        if not is_even:
            send_c(k, deep_in)

    def run_wide(k, is_even, is_end):
        to_mate(k).wait_recv()
        if not is_end:
            for n, (start, size) in enumerate(CUTS):
                term = jnp.dot(
                    wide_in[k], wide_w[:, start:start + size], preferred_element_type=F32
                )
                kept = wide_in[k, :, start:start + size].astype(F32)
                wide_out[k, :, start:start + size] = (kept + SCALE * term).astype(BF16)
                to_outer(k, n).start()
        if is_even:
            send_c(k, wide_in)

    def by_place(work, k, allowed):
        for is_even in (True, False):
            for is_end in (True, False):
                here = jnp.logical_and(even == is_even, at_end == is_end)

                @pl.when(jnp.logical_and(allowed, here))
                def _():
                    work(k, is_even, is_end)

    def each(work):
        @pl.loop(0, MICRO)
        def _(k):
            work(k)

    def gather_sides():
        @pl.when(early)
        def _():
            each(lambda k: c_side(k).start())

        each(widen)

        @pl.when(jnp.logical_not(middle))
        def _():
            each(pass_close)

    def gather_rest():
        each(lambda k: pass_on(c_ring(k, other_hi, 4)))

        def finish(k):
            arrived(c_ring(k, hi, 0))
            arrived(c_ring(k, other_hi, 4))

        each(finish)

    deep_first = (pair < TURN) == even

    def tell(teller, start):
        @pl.when(section == teller)
        def _():
            for told in range(start, start + 8):
                pl.semaphore_signal(passed, inc=1, device_id=(told, dp), device_id_type=MESH)

    gap = jnp.where(pair < TURN, 2 * TURN - 1 - 2 * pair, 2 * pair + 1 - 2 * TURN)
    lag = jnp.minimum(gap * LAG // 4, MICRO)
    deep_lag = jnp.where(deep_first, 0, lag)
    wide_lag = jnp.where(deep_first, lag, 0)

    @pl.loop(0, MICRO + lag)
    def _(t):
        def turn(work, late):
            k = t - late
            allowed = jnp.logical_and(k >= 0, k < MICRO)
            by_place(work, jnp.clip(k, 0, MICRO - 1), allowed)

        turn(run_deep, deep_lag)
        turn(run_wide, wide_lag)

        @pl.when(t == MICRO - 1)
        def _():
            tell(8, 0)
            tell(23, 24)

            @pl.when(plane == 0)
            def _():
                pl.semaphore_wait(passed, 1)
                send_own_x()

            @pl.when(early)
            def _():
                pl.semaphore_wait(passed, 1)
                gather_sides()
                gather_rest()

        @pl.when(t == MICRO + TELL)
        def _():
            tell(7, 8)
            tell(24, 16)

    @pl.when(middle)
    def _():
        each(pass_close)
        pl.semaphore_wait(passed, 1)
        each(lambda k: c_side(k).start())

    @pl.when(plane > 0)
    def _():
        send_own_x()

    @pl.when(jnp.logical_not(early))
    def _():
        gather_sides()

    @pl.when(plane == 0)
    def _():
        gather_rest()

    for index in range(7):
        x_link(index, x_win.at[dp]).wait_recv()

    for g in range(8):
        x_t[:, g * GROUP:(g + 1) * GROUP] = x_win[g].reshape(GROUP, WIN).T
    own_rows = rows(64 * lax.rem(y, 2), ROWS)

    def select(height, width):
        return (
            lax.rem(lax.broadcasted_iota(jnp.int32, (height, width), 0), 64)
            == lax.broadcasted_iota(jnp.int32, (height, width), 1)
        )

    def same_block(size):
        return (
            lax.broadcasted_iota(jnp.int32, (size, size), 0) // 64
            == lax.broadcasted_iota(jnp.int32, (size, size), 1) // 64
        )

    def fold(gram, width=64):
        size = gram.shape[0]
        kept = jnp.where(same_block(size), gram, 0.0)
        return jnp.dot(
            kept, select(size, width).astype(F32), precision=lax.Precision.HIGHEST,
            preferred_element_type=F32,
        )

    def unfold(blocks):
        size = blocks.shape[0]
        tiled = lax.dot_general(
            blocks, select(size, 64).astype(BF16), (((1,), (1,)), ((), ())), preferred_element_type=F32
        )
        return jnp.where(same_block(size), tiled, 0.0).astype(BF16)

    def contract(a, b):
        return lax.dot_general(a, b, (((1,), (1,)), ((), ())), preferred_element_type=F32)

    own = x_t[own_rows, :]
    fac[dp] = fold(contract(own, own) / TOK, 128).astype(BF16)
    shares = []
    for index in range(7):
        one = copy(
            fac.at[dp], fac.at[dp], fac_send.at[index], fac_recv.at[index], peer(index)
        )
        one.start()
        shares.append(one)

    @pl.when(middle)
    def _():
        gather_rest()

    left = unfold(a_inv[...])

    @pl.loop(0, 10)
    def _(n):
        cols = lanes(n * 256, 256)
        c_cols = c_all[:, :, :, cols].reshape(TOK, 256)
        g_out[rows(n * 256, 256), :] = fold(jnp.dot(c_cols.T, c_cols, preferred_element_type=F32) / TOK)
        grad = jnp.dot(x_t[own_rows, :], c_cols, preferred_element_type=F32) / TOK
        halfway = jnp.dot(left, grad.astype(BF16), preferred_element_type=F32).astype(BF16)
        right = unfold(g_inv[rows(n * 256, 256), :])
        step = jnp.dot(halfway, right, preferred_element_type=F32)
        w_out[:, cols] = (w_in[:, cols].astype(F32) - step).astype(BF16)

    for one in shares:
        one.wait()
    for owner in range(8):
        a_out[owner * ROWS:(owner + 1) * ROWS, :] = fac[owner, :, :BLK].astype(F32)

    def close_sends(k):
        to_mate(k).wait_send()
        @pl.when(jnp.logical_not(at_end))
        def _():
            for n in range(len(CUTS)):
                to_outer(k, n).wait_send()

        c_side(k).wait_send()
        sent(c_ring(k, hi, 0))
        sent(c_ring(k, other_hi, 4))

    each(close_sends)
    for index in range(7):
        x_link(index, x_win.at[dp]).wait_send()


def local(inputs, cotangent, weight, a_inv, g_inv):
    vmem = pl.BlockSpec(memory_space=pltpu.VMEM)
    dma = pltpu.SemaphoreType.DMA
    held = pltpu.VMEM((MICRO, M, WD), BF16)
    new_weight, a_fac, g_fac = pl.pallas_call(
        kernel,
        out_shape=(
            jax.ShapeDtypeStruct((ROWS, WD), BF16),
            jax.ShapeDtypeStruct((WD, BLK), F32),
            jax.ShapeDtypeStruct((WD, BLK), F32),
        ),
        in_specs=[vmem] * 5,
        out_specs=(vmem,) * 3,
        scratch_shapes=[
            pltpu.VMEM((WD, WD), BF16),
            pltpu.VMEM((WD, WD), BF16),
            held, held, held, held,
            pltpu.VMEM((M, WD), F32),
            pltpu.VMEM((8, MICRO, M, WIN), BF16),
            pltpu.VMEM((8, MICRO, M, WD), BF16),
            pltpu.VMEM((WIN, TOK), BF16),
            pltpu.VMEM((8, ROWS, 128), BF16),
            dma((14,)), dma((14,)),
            dma((MICRO, len(CUTS))), dma((MICRO, len(CUTS))), dma((MICRO,)), dma((MICRO,)),
            dma((7,)), dma((7,)), dma((MICRO, 9)), dma((MICRO, 9)),
            dma((7,)), dma((7,)), pltpu.SemaphoreType.REGULAR,
        ],
        compiler_params=pltpu.CompilerParams(
            collective_id=0, has_side_effects=True, vmem_limit_bytes=56 << 20
        ),
        cost_estimate=pl.CostEstimate(flops=6 << 30, bytes_accessed=8 << 20, transcendentals=0),
        name="kfac",
    )(
        inputs, cotangent, weight[0],
        a_inv[0].reshape(ROWS, BLK), g_inv[0].reshape(WD, BLK),
    )
    return (
        new_weight[None],
        a_fac.reshape(1, NB, BLK, BLK),
        g_fac.reshape(1, NB, BLK, BLK),
    )


def solution(mesh):
    placed = (
        P(None, "dp", None),
        P(None, "dp", None),
        P("section", "dp", None),
        P("section", "dp", None, None),
        P("section", None, None, None),
    )
    return jax.shard_map(
        local,
        mesh=mesh,
        in_specs=placed,
        out_specs=(
            P("section", "dp", None),
            P("section", None, None, None),
            P("section", None, None, None),
        ),
        check_vma=False,
    )
```

```python
import functools
import math

import jax
import jax.numpy as jnp
from jax import lax
from jax.experimental import pallas as pl
from jax.experimental.pallas import tpu as pltpu
from jax.sharding import PartitionSpec as P

MESH = pl.DeviceIdType.MESH
F32 = jnp.float32
BF16 = jnp.bfloat16
WD = 2560
ROWS = WD // 8
BLK = 64
NB = 40
WIN = 384
MICRO = 4
M = 32
GROUP = MICRO * M
TOK = 8 * GROUP
SCALE = 0.25 / math.sqrt(WD)
SECTIONS = 32
TURN = 8
LAG = 10
TELL = 2
CUTS = tuple((start, 512) for start in range(0, WD, 512))


def lanes(start, size):
    return pl.ds(pl.multiple_of(start, 128), size)


def rows(start, size):
    return pl.ds(pl.multiple_of(start, 64), size)


def kernel(
    x_in, c_in, w_in, a_inv, g_inv,
    w_out, a_out, g_out,
    deep_w, wide_w, deep_in, wide_in, deep_out, wide_out, acc,
    x_win, c_all, x_t, fac, left_w, right_w,
    gat_send, gat_recv, deep_send, deep_recv, wide_send, wide_recv,
    x_send, x_recv, c_send, c_recv, fac_send, fac_recv, passed,
):
    section = lax.axis_index("section")
    dp = lax.axis_index("dp")
    core = lax.rem(section, 2)
    pair = section // 2
    plane = section // 8
    early = plane == 3
    middle = jnp.logical_and(plane > 0, plane < 3)
    hi = dp // 4
    y = lax.rem(dp, 4)
    other_hi = 1 - hi
    beside = 4 * other_hi + y
    mate = section + 1 - 2 * core
    outer = section - 1 + 2 * core
    at_end = jnp.logical_or(outer < 0, outer >= SECTIONS)
    even = core == 0

    def across(step):
        return lax.rem(y + step, 4)

    def copy(src, dst, send, recv, target):
        return pltpu.make_async_remote_copy(
            src_ref=src, dst_ref=dst, send_sem=send, recv_sem=recv,
            device_id=target, device_id_type=MESH,
        )

    def peer(index):
        if index < 4:
            return (section, 4 * other_hi + across(index))
        return (section, 4 * hi + across(index - 3))

    barrier = pltpu.get_barrier_semaphore()

    def greet(target):
        pl.semaphore_signal(barrier, inc=1, device_id=target, device_id_type=MESH)

    for index in range(7):
        greet(peer(index))
    greet((mate, dp))
    teller = jnp.where(plane == 0, 8, jnp.where(plane == 1, 7, jnp.where(plane == 2, 24, 23)))
    telling = jnp.logical_or(
        jnp.logical_or(section == 7, section == 8), jnp.logical_or(section == 23, section == 24)
    )

    @pl.when(teller != outer)
    def _():
        greet((teller, dp))

    @pl.when(jnp.logical_not(at_end))
    def _():
        greet((outer, dp))

    pl.semaphore_wait(barrier, 8 + jnp.where(at_end, 0, 1) + jnp.where(telling, 7, 0))

    ahead, behind = across(1), across(3)

    def ring(view, own, send, recv):
        def to(target_y, slot, ref, place):
            return copy(ref, place, send(slot), recv(slot), (section, 4 * hi + target_y))

        def link(slot):
            if slot < 2:
                return to((ahead, behind)[slot], slot, own, view(y))
            passed = view((behind, ahead)[slot - 2], slot - 2)
            return to((ahead, behind)[slot - 2], slot, passed, passed)

        return link

    def pass_on(links):
        links(0).wait_recv()
        links(2).start()
        links(1).wait_recv()
        links(3).start()

    def arrived(links):
        links(2).wait_recv()
        links(3).wait_recv()

    def sent(links):
        for slot in range(4):
            links(slot).wait_send()

    def select(height, width):
        return (
            lax.rem(lax.broadcasted_iota(jnp.int32, (height, width), 0), 64)
            == lax.broadcasted_iota(jnp.int32, (height, width), 1)
        )

    def same_block(size):
        return (
            lax.broadcasted_iota(jnp.int32, (size, size), 0) // 64
            == lax.broadcasted_iota(jnp.int32, (size, size), 1) // 64
        )

    def fold(gram, width=64):
        size = gram.shape[0]
        kept = jnp.where(same_block(size), gram, 0.0)
        return jnp.dot(
            kept, select(size, width).astype(F32), precision=lax.Precision.HIGHEST,
            preferred_element_type=F32,
        )

    def unfold(blocks):
        size = blocks.shape[0]
        tiled = lax.dot_general(
            blocks, select(size, 64).astype(BF16), (((1,), (1,)), ((), ())), preferred_element_type=F32
        )
        return jnp.where(same_block(size), tiled, 0.0).astype(BF16)

    def lay_out_inverses():
        left_w[...] = unfold(a_inv[...])

        @pl.loop(0, 10)
        def _(n):
            right_w[n] = unfold(g_inv[rows(n * 256, 256), :])

    def gather_weight(full, flipped):
        def block(group, low, size):
            def view(owner, part=None):
                start = (4 * group + owner) * ROWS + low
                if part is None:
                    return full.at[pl.ds(pl.multiple_of(start, 32), size), :]
                half = size // 2
                return full.at[pl.ds(pl.multiple_of(start + part * half, 16), half), :]

            return view

        def links_of(view, own, base):
            return ring(
                view, own, lambda slot: gat_send.at[base + slot], lambda slot: gat_recv.at[base + slot]
            )

        half = ROWS // 2
        sides, rings = [], []
        for part in range(2):
            there = block(hi, part * half, half)(y)
            sides.append(copy(
                w_in.at[pl.ds(part * half, half), :], there,
                gat_send.at[12 + part], gat_recv.at[12 + part], (section, beside),
            ))
            sides[-1].start()
        close = links_of(block(hi, 0, ROWS), w_in, 0)
        close(0).start()
        close(1).start()
        full[rows(dp * ROWS, ROWS), :] = w_in[...]
        lay_out_inverses()
        for part in range(2):
            view = block(other_hi, part * half, half)
            rings.append(links_of(view, view(y), 4 + 4 * part))

        def turn(group):
            for n in range(5):
                cols = lanes(group * 4 * ROWS + n * 256, 256)
                flipped[:, cols] = full[rows(group * 4 * ROWS + n * 256, 256), :].T

        sides[0].wait_recv()
        rings[0](0).start()
        rings[0](1).start()
        pass_on(close)
        sides[1].wait_recv()
        rings[1](0).start()
        rings[1](1).start()
        arrived(close)
        turn(hi)
        pass_on(rings[0])
        pass_on(rings[1])
        arrived(rings[0])
        arrived(rings[1])
        turn(other_hi)
        for one in sides:
            one.wait_send()
        for links in (close, rings[0], rings[1]):
            sent(links)

    @pl.when(even)
    def _():
        gather_weight(deep_w, wide_w)

    @pl.when(jnp.logical_not(even))
    def _():
        gather_weight(wide_w, deep_w)

    @pl.when(jnp.logical_and(at_end, even))
    def _():
        deep_in[...] = x_in[...]

    @pl.when(jnp.logical_and(at_end, jnp.logical_not(even)))
    def _():
        deep_in[...] = c_in[...]

    def to_mate(k):
        return copy(deep_out.at[k], wide_in.at[k], wide_send.at[k], wide_recv.at[k], (mate, dp))

    def to_outer(k, n):
        view = (k, slice(None), pl.ds(*CUTS[n]))
        return copy(
            wide_out.at[view], deep_in.at[view], deep_send.at[k, n], deep_recv.at[k, n], (outer, dp)
        )

    def window(owner):
        return 320 * owner - 64 * lax.rem(owner, 2)

    def x_link(index, source):
        return copy(source, x_win.at[dp], x_send.at[index], x_recv.at[index], peer(index))

    def send_x(source):
        for index in range(7):
            start = window(peer(index)[1])
            x_link(index, source.at[:, :, lanes(start, WIN)]).start()
        x_win[dp] = source[:, :, lanes(window(dp), WIN)]

    def send_own_x():
        @pl.when(even)
        def _():
            send_x(deep_in)

        @pl.when(jnp.logical_not(even))
        def _():
            send_x(wide_in)

    def c_ring(k, group, base):
        def view(owner, part=None):
            if part is None:
                return c_all.at[4 * group + owner, k]
            return c_all.at[4 * group + owner, k, :, pl.ds(part * (WD // 2), WD // 2)]

        return ring(
            view, view(y), lambda slot: c_send.at[k, base + slot], lambda slot: c_recv.at[k, base + slot]
        )

    def c_side(k):
        view = c_all.at[dp, k]
        return copy(view, view, c_send.at[k, 8], c_recv.at[k, 8], (section, beside))

    def send_c(k, source):
        c_all[dp, k] = source[k]
        links = c_ring(k, hi, 0)
        links(0).start()
        links(1).start()

        @pl.when(plane == 0)
        def _():
            c_side(k).start()

    def widen(k):
        c_side(k).wait_recv()
        links = c_ring(k, other_hi, 4)
        links(0).start()
        links(1).start()

    def pass_close(k):
        pass_on(c_ring(k, hi, 0))

    def run_deep(k, is_even, is_end):
        for n, (start, size) in enumerate(CUTS):
            if not is_end:
                to_outer(k, n).wait_recv()
            term = jnp.dot(
                deep_in[k, :, start:start + size], deep_w[start:start + size, :],
                preferred_element_type=F32,
            )
            if n == 0:
                acc[...] = term
            else:
                acc[...] += term
        deep_out[k] = (deep_in[k].astype(F32) + SCALE * acc[...]).astype(BF16)
        to_mate(k).start()
        if not is_even:
            send_c(k, deep_in)

    def run_wide(k, is_even, is_end):
        to_mate(k).wait_recv()
        if not is_end:
            for n, (start, size) in enumerate(CUTS):
                term = jnp.dot(
                    wide_in[k], wide_w[:, start:start + size], preferred_element_type=F32
                )
                kept = wide_in[k, :, start:start + size].astype(F32)
                wide_out[k, :, start:start + size] = (kept + SCALE * term).astype(BF16)
                to_outer(k, n).start()
        if is_even:
            send_c(k, wide_in)

    def by_place(work, k, allowed):
        for is_even in (True, False):
            for is_end in (True, False):
                here = jnp.logical_and(even == is_even, at_end == is_end)

                @pl.when(jnp.logical_and(allowed, here))
                def _():
                    work(k, is_even, is_end)

    def each(work):
        @pl.loop(0, MICRO)
        def _(k):
            work(k)

    def gather_sides():
        @pl.when(early)
        def _():
            each(lambda k: c_side(k).start())

        each(widen)

        @pl.when(jnp.logical_not(middle))
        def _():
            each(pass_close)

    def gather_rest():
        each(lambda k: pass_on(c_ring(k, other_hi, 4)))

        def finish(k):
            arrived(c_ring(k, hi, 0))
            arrived(c_ring(k, other_hi, 4))

        each(finish)

    deep_first = (pair < TURN) == even

    def tell(teller, start):
        @pl.when(section == teller)
        def _():
            for told in range(start, start + 8):
                pl.semaphore_signal(passed, inc=1, device_id=(told, dp), device_id_type=MESH)

    gap = jnp.where(pair < TURN, 2 * TURN - 1 - 2 * pair, 2 * pair + 1 - 2 * TURN)
    lag = jnp.minimum(gap * LAG // 4, MICRO)
    deep_lag = jnp.where(deep_first, 0, lag)
    wide_lag = jnp.where(deep_first, lag, 0)

    @pl.loop(0, MICRO + lag)
    def _(t):
        def turn(work, late):
            k = t - late
            allowed = jnp.logical_and(k >= 0, k < MICRO)
            by_place(work, jnp.clip(k, 0, MICRO - 1), allowed)

        turn(run_deep, deep_lag)
        turn(run_wide, wide_lag)

        @pl.when(t == MICRO - 1)
        def _():
            tell(8, 0)
            tell(23, 24)

            @pl.when(plane == 0)
            def _():
                pl.semaphore_wait(passed, 1)
                send_own_x()

            @pl.when(early)
            def _():
                pl.semaphore_wait(passed, 1)
                gather_sides()
                gather_rest()

        @pl.when(t == MICRO + TELL)
        def _():
            tell(7, 8)
            tell(24, 16)

    @pl.when(middle)
    def _():
        each(pass_close)
        pl.semaphore_wait(passed, 1)
        each(lambda k: c_side(k).start())

    @pl.when(plane > 0)
    def _():
        send_own_x()

    @pl.when(jnp.logical_not(early))
    def _():
        gather_sides()

    @pl.when(plane == 0)
    def _():
        gather_rest()

    for index in range(7):
        x_link(index, x_win.at[dp]).wait_recv()

    for g in range(8):
        x_t[:, g * GROUP:(g + 1) * GROUP] = x_win[g].reshape(GROUP, WIN).T
    own_rows = rows(64 * lax.rem(y, 2), ROWS)

    def contract(a, b):
        return lax.dot_general(a, b, (((1,), (1,)), ((), ())), preferred_element_type=F32)

    own = x_t[own_rows, :]
    fac[dp] = fold(contract(own, own) / TOK, 128).astype(BF16)
    shares = []
    for index in range(7):
        one = copy(
            fac.at[dp], fac.at[dp], fac_send.at[index], fac_recv.at[index], peer(index)
        )
        one.start()
        shares.append(one)

    @pl.when(middle)
    def _():
        gather_rest()


    @pl.loop(0, 10)
    def _(n):
        cols = lanes(n * 256, 256)
        c_cols = c_all[:, :, :, cols].reshape(TOK, 256)
        g_out[rows(n * 256, 256), :] = fold(jnp.dot(c_cols.T, c_cols, preferred_element_type=F32) / TOK)
        grad = jnp.dot(x_t[own_rows, :], c_cols, preferred_element_type=F32) / TOK
        halfway = jnp.dot(left_w[...], grad.astype(BF16), preferred_element_type=F32).astype(BF16)
        step = jnp.dot(halfway, right_w[n], preferred_element_type=F32)
        w_out[:, cols] = (w_in[:, cols].astype(F32) - step).astype(BF16)

    for one in shares:
        one.wait()
    for owner in range(8):
        a_out[owner * ROWS:(owner + 1) * ROWS, :] = fac[owner, :, :BLK].astype(F32)

    def close_sends(k):
        to_mate(k).wait_send()
        @pl.when(jnp.logical_not(at_end))
        def _():
            for n in range(len(CUTS)):
                to_outer(k, n).wait_send()

        c_side(k).wait_send()
        sent(c_ring(k, hi, 0))
        sent(c_ring(k, other_hi, 4))

    each(close_sends)
    for index in range(7):
        x_link(index, x_win.at[dp]).wait_send()


def local(inputs, cotangent, weight, a_inv, g_inv):
    vmem = pl.BlockSpec(memory_space=pltpu.VMEM)
    dma = pltpu.SemaphoreType.DMA
    held = pltpu.VMEM((MICRO, M, WD), BF16)
    new_weight, a_fac, g_fac = pl.pallas_call(
        kernel,
        out_shape=(
            jax.ShapeDtypeStruct((ROWS, WD), BF16),
            jax.ShapeDtypeStruct((WD, BLK), F32),
            jax.ShapeDtypeStruct((WD, BLK), F32),
        ),
        in_specs=[vmem] * 5,
        out_specs=(vmem,) * 3,
        scratch_shapes=[
            pltpu.VMEM((WD, WD), BF16),
            pltpu.VMEM((WD, WD), BF16),
            held, held, held, held,
            pltpu.VMEM((M, WD), F32),
            pltpu.VMEM((8, MICRO, M, WIN), BF16),
            pltpu.VMEM((8, MICRO, M, WD), BF16),
            pltpu.VMEM((WIN, TOK), BF16),
            pltpu.VMEM((8, ROWS, 128), BF16),
            pltpu.VMEM((ROWS, ROWS), BF16),
            pltpu.VMEM((10, 256, 256), BF16),
            dma((14,)), dma((14,)),
            dma((MICRO, len(CUTS))), dma((MICRO, len(CUTS))), dma((MICRO,)), dma((MICRO,)),
            dma((7,)), dma((7,)), dma((MICRO, 9)), dma((MICRO, 9)),
            dma((7,)), dma((7,)), pltpu.SemaphoreType.REGULAR,
        ],
        compiler_params=pltpu.CompilerParams(
            collective_id=0, has_side_effects=True, vmem_limit_bytes=56 << 20
        ),
        cost_estimate=pl.CostEstimate(flops=6 << 30, bytes_accessed=8 << 20, transcendentals=0),
        name="kfac",
    )(
        inputs, cotangent, weight[0],
        a_inv[0].reshape(ROWS, BLK), g_inv[0].reshape(WD, BLK),
    )
    return (
        new_weight[None],
        a_fac.reshape(1, NB, BLK, BLK),
        g_fac.reshape(1, NB, BLK, BLK),
    )


def solution(mesh):
    placed = (
        P(None, "dp", None),
        P(None, "dp", None),
        P("section", "dp", None),
        P("section", "dp", None, None),
        P("section", None, None, None),
    )
    return jax.shard_map(
        local,
        mesh=mesh,
        in_specs=placed,
        out_specs=(
            P("section", "dp", None),
            P("section", None, None, None),
            P("section", None, None, None),
        ),
        check_vma=False,
    )
```
